256 devices in a mesh: chan: 8 (over x_lo, y), ctx: 32 (over x_hi, z, core).
Axes of the slice: x: 4 (x_hi: 2, x_lo: 2; x = x_hi * 2 + x_lo), y: 4, z: 8, core: 2. Of those that a mesh axis runs over, the one named last changes fastest.
Arguments:
- inputs: bfloat16 [4096, 8192], P('ctx', 'chan'), may hold values from -6 to 6
- w_value: bfloat16 [8192, 4096], P('ctx', 'chan'), may hold values from -0.125 to 0.125
- q_field: bfloat16 [4096, 4096], P('ctx', 'chan'), may hold values from -6 to 6
- k_field: bfloat16 [4096, 4096], P('ctx', 'chan'), may hold values from -6 to 6
- filters: float32 [128, 4096], P(None, 'chan'), may hold values from -1.2 to 1.2
- out_grad: bfloat16 [4096, 4096], P('ctx', 'chan'), may hold values from -6 to 6
Outputs:
- in_grad: bfloat16 [4096, 8192], P('ctx', 'chan')
- w_grad: bfloat16 [8192, 4096], P('ctx', 'chan')
- q_grad: bfloat16 [4096, 4096], P('ctx', 'chan')
- k_grad: bfloat16 [4096, 4096], P('ctx', 'chan')
- filter_grad: float32 [128, 4096], P(None, 'chan')
The draws below stay inside these ranges and needn't reach their ends.
All inputs are finite; a program needn't handle non-finite values.
Results may differ from the reference program's by a relative error of at most 0.033.
Values may be sent and summed in bfloat16 or wider, within the bound.
A program may use at most 64 MiB of HBM per device.

```python
import jax
import jax.numpy as jnp
from jax import lax

D = 8192
C = 4096
TAPS = 128
TOK_DEV = 128
TOKENS = 4096
N_CHAN = 8
N_CTX = 32


def draw_filters(key, part):
    key = jax.random.fold_in(key, 11)
    rate_key, base_key = jax.random.split(key)
    rates = jnp.exp(jax.random.uniform(rate_key, (1, C), jnp.float32, jnp.log(0.004), jnp.log(0.12)))
    tap_pos = jnp.arange(TAPS, dtype=jnp.float32)[:, None]
    base = jnp.clip(jax.random.normal(base_key, (TAPS, C), jnp.float32), -4.0, 4.0)
    return 0.3 * base * jnp.exp(-tap_pos * rates)


def spiked(array, own_key, source, target, parts, factor):
    def block_of(position):
        return (jnp.arange(array.shape[position]) // (array.shape[position] // parts)).reshape((-1,) + (1,) * (array.ndim - 1 - position))

    first = jax.random.permutation(own_key, parts)[block_of(target)]
    far = (block_of(target) + parts // 2) % parts
    return jnp.where((block_of(source) == first) | (block_of(source) == far), factor * array, array)


def steps_of(own_key, dims, cuts, smallest, top_value):
    def one(position, blocks):
        heights = jax.random.uniform(jax.random.fold_in(jax.random.fold_in(own_key, 6), position), (blocks,), jnp.float32, smallest / len(cuts), top_value / len(cuts))
        return jnp.repeat(jnp.exp(heights), dims[position] // blocks).reshape((-1,) + (1,) * (len(dims) - position - 1))

    level = one(*cuts[0])
    for cut in cuts[1:]:
        level = level * one(*cut)
    return level


def noise(key, dims, scale, bound, cuts=(), kind=jnp.bfloat16):
    level = steps_of(key, dims, cuts, -0.22, 0.18) if cuts else 1.0
    array = jax.random.normal(key, dims, jnp.float32) * scale * level
    return jnp.minimum(jnp.maximum(array, -bound), bound).astype(kind)


def bell_draw_with(key, shape, spread, bound, cuts, heavy, held_as=jnp.bfloat16):
    drawn = spread * jax.random.normal(key, shape, jnp.float32)
    if cuts:
        drawn = drawn * steps_of(key, shape, cuts, -0.22, 0.18)
    return jnp.clip(spiked(drawn, jax.random.fold_in(key, 3), *heavy), -bound, bound).astype(held_as)


def setup_inputs(seed: int = 0) -> dict:
    keys = jax.random.split(jax.random.key(seed), 7)
    return {
        "inputs": bell_draw_with(keys[0], (TOKENS, D), 1.0, 6.0, ((0, 32), (1, 8)), (0, 1, 32, 2.75)),
        "w_value": bell_draw_with(keys[1], (D, C), D ** -0.5, 0.125, ((0, 32), (1, 8)), (1, 0, 32, 2.75)),
        "q_field": noise(keys[2], (TOKENS, C), 1.0, 6.0, ((0, 32), (1, 8))),
        "k_field": noise(keys[3], (TOKENS, C), 1.0, 6.0, ((0, 32), (1, 8))),
        "filters": draw_filters(jax.random.fold_in(keys[6], 71), 0),
        "out_grad": noise(keys[5], (TOKENS, C), 1.0, 6.0, ((0, 32), (1, 8))),
    }


def tap_sums(filters, fwd_ext, bwd_ext, grad_h32, rows):
    taps = filters.shape[0]
    width = taps - 1
    group = 8
    chans = filters.shape[1]

    def step_fn(block_index, carry):
        forward, adjoint, filter_part = carry
        rows_part = []
        for offset in range(group):
            tap = block_index * group + offset
            coeff = lax.dynamic_slice_in_dim(filters, tap, 1, 0)
            shifted = lax.dynamic_slice_in_dim(fwd_ext, width - tap, rows, 0)
            ahead = lax.dynamic_slice_in_dim(bwd_ext, tap, rows, 0)
            forward = forward + coeff * shifted
            adjoint = adjoint + coeff * ahead
            rows_part.append(jnp.sum(grad_h32 * shifted, axis=0, keepdims=True))
        filter_part = lax.dynamic_update_slice_in_dim(filter_part, jnp.concatenate(rows_part, 0), block_index * group, 0)
        return forward, adjoint, filter_part

    start = (jnp.zeros((rows, chans), jnp.float32), jnp.zeros((rows, chans), jnp.float32), jnp.zeros((taps, chans), jnp.float32))
    return lax.fori_loop(0, taps // group, step_fn, start)


def reference(inputs, w_value, q_field, k_field, filters, out_grad):
    width = TAPS - 1
    values = jnp.dot(inputs, w_value, preferred_element_type=jnp.float32).astype(jnp.bfloat16)
    gated = (k_field.astype(jnp.float32) * values.astype(jnp.float32)).astype(jnp.bfloat16)
    grad_h = (out_grad.astype(jnp.float32) * q_field.astype(jnp.float32)).astype(jnp.bfloat16)
    edge_zeros = jnp.zeros((width, C), jnp.float32)
    fwd_ext = jnp.concatenate([edge_zeros, gated.astype(jnp.float32)], 0)
    grad_h32 = grad_h.astype(jnp.float32)
    bwd_ext = jnp.concatenate([grad_h32, edge_zeros], 0)
    filtered, grad_g, filter_grad = tap_sums(filters, fwd_ext, bwd_ext, grad_h32, TOKENS)
    q_grad = (out_grad.astype(jnp.float32) * filtered).astype(jnp.bfloat16)
    k_grad = (grad_g * values.astype(jnp.float32)).astype(jnp.bfloat16)
    v_grad = (grad_g * k_field.astype(jnp.float32)).astype(jnp.bfloat16)
    group_width = C // N_CHAN
    grad_groups = jnp.transpose(v_grad.reshape(TOKENS, N_CHAN, group_width), (1, 0, 2))
    weight_groups = jnp.transpose(w_value.reshape(D, N_CHAN, group_width), (1, 0, 2))

    def add_group(total, pair):
        group_grad, group_weight = pair
        term = lax.dot_general(group_grad, group_weight, (((1,), (1,)), ((), ())), preferred_element_type=jnp.float32)
        return total + term.astype(jnp.bfloat16).astype(jnp.float32), None

    in_total, unused = lax.scan(add_group, jnp.zeros((TOKENS, D), jnp.float32), (grad_groups, weight_groups))
    input_blocks = inputs.reshape(N_CTX, TOK_DEV, D)
    grad_blocks = v_grad.reshape(N_CTX, TOK_DEV, C)

    def add_block(total, pair):
        block_in, block_grad = pair
        term = lax.dot_general(block_in, block_grad, (((0,), (0,)), ((), ())), preferred_element_type=jnp.float32)
        return total + term.astype(jnp.bfloat16).astype(jnp.float32), None

    w_total, unused_two = lax.scan(add_block, jnp.zeros((D, C), jnp.float32), (input_blocks, grad_blocks))
    return in_total.astype(jnp.bfloat16), w_total.astype(jnp.bfloat16), q_grad, k_grad, filter_grad
```

```python
import jax
import jax.numpy as jnp
import ml_dtypes
import numpy as np
from jax import lax
from jax.experimental import pallas as pl
from jax.experimental.pallas import tpu as pltpu
from jax.sharding import PartitionSpec as P

MESH = pl.DeviceIdType.MESH
F32, BF16 = jnp.float32, jnp.bfloat16
BLK = 128
CH = 512
NX, NY, NZ = 2, 4, 8
N_CTX = 2 * NZ * 2

R_IN1, R_IN2, R_W, R_WX = 0, 8, 11, 25
R_H, R_G, R_V, R_VC, R_VX = 26, 27, 28, 35, 39
R_RS, R_IG1, R_IG2, R_WG = 42, 56, 59, 67
R_F1, R_F2, R_F3, R_F4 = 68, 71, 78, 85
N_RECV = 88
N_SEND = 110
N_LOCAL = 16


def transforms():
    k, n = np.arange(BLK)[:, None], np.arange(BLK)[None, :]
    angle = np.pi * (2 * k + 1) * n / (2 * BLK)
    full = np.concatenate([np.cos(angle), -np.sin(angle)], 0)
    high = full.astype(ml_dtypes.bfloat16)
    low = (full - high.astype(np.float64)).astype(ml_dtypes.bfloat16)
    forward = np.concatenate([high, low], 0)
    inverse = np.concatenate([high.T, low.T], 0).astype(np.float32) / BLK
    return forward, inverse.astype(ml_dtypes.bfloat16)


def kernel(
    x_hbm, w_hbm, q_hbm, k_hbm, f_hbm, o_hbm, fwd_hbm, inv_hbm,
    ig_hbm, wg_hbm, qg_hbm, kg_hbm, fg_hbm,
    q_v, k_v, o_v, f_v, fwd_v, inv_v,
    h_v, hn_v, g_v, gp_v, fs_v, hs_v, gg_v,
    gin, wfull, vfull,
    rs_out, rs_in,
    val_t, val_s, val_c, val_xs, val_xr,
    ig_s, ig_r, ig_sum,
    qg_v, kg_v, fq_s, fq_r, fz_s, fz_r, fz_all, fq_all, fg_v,
    wg_own, wg_par,
    ssem, rsem, lsem,
):
    chan, ctx = lax.axis_index("chan"), lax.axis_index("ctx")
    xl, y = chan // NY, chan % NY
    xh, z, core = ctx // (2 * NZ), (ctx // 2) % NZ, ctx % 2
    tb = xh * 2 + core
    xo = 1 - xl

    def dev(xh_, xl_, y_, z_, core_):
        return (xl_ * NY + y_, xh_ * (2 * NZ) + z_ * 2 + core_)

    def plane(d):
        return dev((xh + d // 4) % 2, (xl + (d // 2) % 2) % 2, y, z, (core + d % 2) % 2)

    def y_peer(d):
        return dev(xh, xl, (y + d) % NY, z, core)

    def z_peer(d):
        return dev(xh, xl, y, (z + d + NZ) % NZ, core)

    def ctx_peer(d):
        return (chan, (ctx + d + N_CTX) % N_CTX)

    right, left, partner = z_peer(1), z_peer(-1), plane(2)
    started = []
    local_ids = iter(range(N_LOCAL))

    def send(src, dst, device, recv):
        copy = pltpu.make_async_remote_copy(
            src_ref=src, dst_ref=dst, send_sem=ssem.at[len(started)], recv_sem=rsem.at[recv],
            device_id=device, device_id_type=MESH,
        )
        copy.start()
        started.append(copy)

    def arrive(dst, recv):
        pltpu.make_async_copy(dst, dst, rsem.at[recv]).wait()

    def local(src, dst):
        copy = pltpu.make_async_copy(src, dst, lsem.at[next(local_ids)])
        copy.start()
        return copy

    def rows(index, size=BLK):
        return pl.ds(pl.multiple_of(index * size, size), size)

    def dot(a, b):
        return jnp.dot(a, b, preferred_element_type=F32)

    loads = [local(a, b) for a, b in (
        (o_hbm, o_v), (q_hbm, q_v), (fwd_hbm, fwd_v), (f_hbm, f_v), (inv_hbm, inv_v), (k_hbm, k_v))]
    w_local = local(w_hbm.at[rows(xl), :], wfull.at[xl, rows(z), :])
    barrier = pltpu.get_barrier_semaphore()
    greeted = [plane(d) for d in range(1, 8)] + [y_peer(d) for d in range(1, NY)]
    greeted += [z_peer(d) for d in range(1, NZ)] + [ctx_peer(1), ctx_peer(-1)]
    for device in greeted:
        pl.semaphore_signal(barrier, inc=1, device_id=device, device_id_type=MESH)
    pl.semaphore_wait(barrier, len(greeted))

    def w_piece(half, zz):
        return wfull.at[half, rows(zz), :]

    send(w_hbm.at[rows(xl), :], w_piece(xl, z), right, R_W + 0)
    send(w_hbm.at[rows(xl), :], w_piece(xl, z), left, R_W + 7)
    send(w_hbm.at[rows(xo), :], w_piece(xl, z), partner, R_WX)

    def in_slab(b9, xl_, core_):
        return pl.ds(pl.multiple_of(b9 * 512 + core_ * 256 + xl_ * 128, 128), 128)

    def gin_slab(b9):
        return gin.at[rows(tb), pl.ds(pl.multiple_of(y * 256 + b9 * 128, 128), 128)]

    self_sends = []
    for a in range(2):
        for b in range(2):
            xl_d, core_d = (xl + a) % 2, (core + b) % 2
            for b9 in range(2):
                src = x_hbm.at[:, in_slab(b9, xl_d, core_d)]
                if a == 0 and b == 0:
                    far = pltpu.make_async_remote_copy(
                        src_ref=src, dst_ref=gin_slab(b9), send_sem=ssem.at[N_SEND - 1 - b9],
                        recv_sem=rsem.at[R_IN1 + tb * 2 + b9],
                        device_id=dev(xl, xl_d, y, z, core_d), device_id_type=MESH,
                    )
                    near = pltpu.make_async_copy(src, gin_slab(b9), rsem.at[R_IN1 + tb * 2 + b9])

                    @pl.when(xh != xl)
                    def _():
                        far.start()

                    @pl.when(xh == xl)
                    def _():
                        near.start()

                    self_sends.append(far)
                else:
                    send(src, gin_slab(b9), dev(xl, xl_d, y, z, core_d), R_IN1 + tb * 2 + b9)

    loads[0].wait()
    loads[1].wait()
    h = (o_v[...].astype(F32) * q_v[...].astype(F32)).astype(BF16)
    h_v[...] = h
    send(h_v, hn_v, ctx_peer(-1), R_H)

    def forward(block):
        t = dot(fwd_v[...], block)
        return t[:256] + t[256:]

    def inverse(re, im):
        spec = jnp.concatenate([re, im], 0)
        high = spec.astype(BF16)
        low = (spec - high.astype(F32)).astype(BF16)
        t = dot(inv_v[...], high)
        return t[:BLK] + t[BLK:] + dot(inv_v[:BLK], low)

    sign = (1 - 2 * (lax.broadcasted_iota(jnp.int32, (BLK, CH), 0) % 2)).astype(F32)
    loads[2].wait()
    loads[3].wait()
    taps = f_v[...]
    taps_high = taps.astype(BF16)
    taps_low = (taps - taps_high.astype(F32)).astype(BF16)
    fs_v[...] = forward(taps_high) + dot(fwd_v[:256], taps_low)
    hs_v[...] = forward(h)

    w_local.wait()
    arrive(w_piece(xo, z), R_WX)
    send(w_piece(xo, z), w_piece(xo, z), right, R_W + 1)
    send(w_piece(xo, z), w_piece(xo, z), left, R_W + 8)

    def w_from_left(i, forward_on=True):
        half = xl if i % 2 == 0 else xo
        piece = w_piece(half, (z - (i // 2 + 1) + NZ) % NZ)
        arrive(piece, R_W + i)
        if i < 5:
            send(piece, piece, right, R_W + i + 2)

    def w_from_right(i):
        half = xo if i % 2 == 1 or i == 6 else xl
        piece = w_piece(half, (z + (i // 2 + 1)) % NZ)
        arrive(piece, R_W + 7 + i)
        if i < 4:
            send(piece, piece, left, R_W + 7 + i + 2)
        elif i == 5:
            send(piece, piece, left, R_W + 7 + 6)

    w_from_left(0)
    w_from_right(0)

    for i in range(4):
        for b9 in range(2):
            arrive(gin.at[rows(i), pl.ds(pl.multiple_of(y * 256 + b9 * 128, 128), 128)], R_IN1 + i * 2 + b9)

    def gin_cols(yy):
        return gin.at[:, pl.ds(pl.multiple_of(yy * 256, 256), 256)]

    for d in range(1, NY):
        send(gin_cols(y), gin_cols(y), y_peer(d), R_IN2 + d - 1)

    arrive(hn_v, R_H)
    last = ctx == N_CTX - 1
    loads[4].wait()
    loads[5].wait()
    hn = forward(jnp.where(last, jnp.zeros_like(h), hn_v[...]))
    hr = hs_v[:BLK] + sign * hn[BLK:]
    hi = hs_v[BLK:] - sign * hn[:BLK]
    fr, fi = fs_v[:BLK], fs_v[BLK:]
    g_grad = inverse(fr * hr + fi * hi, fr * hi - fi * hr)
    gg_v[...] = g_grad
    mine = vfull.at[xl, rows(tb), :]
    vfull[xl, rows(tb), :] = (g_grad * k_v[...].astype(F32)).astype(BF16)
    for d in (4, 6, 2, 5, 7, 3, 1):
        send(mine, mine, plane(d), R_V + d - 1)

    for i in range(1, 3):
        w_from_left(i)
        w_from_right(i)

    for d in range(1, 8):
        xh_s, xl_s, core_s = (xh + d // 4) % 2, (xl + (d // 2) % 2) % 2, (core + d % 2) % 2
        arrive(vfull.at[xl_s, rows(xh_s * 2 + core_s), :], R_V + d - 1)
    for d in range(1, NY):
        arrive(gin_cols((y - d + NY) % NY), R_IN2 + d - 1)

    def w_term(zz, half):
        part = gin[:, pl.ds(pl.multiple_of(zz * 128, 128), 128)]
        return lax.dot_general(part, vfull[half], (((0,), (0,)), ((), ())), preferred_element_type=F32)

    def rs_step(i):
        hop = 4 - (i + 1) // 2
        for way, device, step in ((0, right, 1), (1, left, -1)):
            half = xl if (i + way) % 2 == 0 else xo
            term = w_term((z + step * hop + NZ) % NZ, half)
            if i >= 2:
                arrive(rs_in.at[way, i - 2], R_RS + way * 7 + i - 2)
                term = term + rs_in[way, i - 2].astype(F32)
            rs_out[way, i] = term.astype(BF16)
            send(rs_out.at[way, i], rs_in.at[way, i], device, R_RS + way * 7 + i)

    rs_step(0)
    rs_step(1)
    for i in range(3, 6):
        w_from_left(i)
        w_from_right(i)
    w_from_left(6)
    w_from_right(6)

    for j in (1, 2, 3, 0):
        xh_d, xl_d = (xh + j // 2) % 2, (xl + j % 2) % 2
        val_t[j] = dot(gin[rows(xh_d, 256), :], wfull[xl_d])
        val_s[j] = val_t[j, rows(1 - core), :].astype(BF16)
        send(val_s.at[j], val_c.at[j], plane(1), R_VC + j)
    rs_step(2)
    for j in (1, 2, 3):
        arrive(val_c.at[j], R_VC + j)
        val_xs[j - 1] = (val_t[j, rows(core), :] + val_c[j].astype(F32)).astype(BF16)
        send(val_xs.at[j - 1], val_xr.at[j - 1], plane(2 * j), R_VX + j - 1)

    def in_term(yy):
        total = 0.0
        for half in range(2):
            total = total + lax.dot_general(
                vfull[half], wfull[half, rows(yy, 256), :], (((1,), (1,)), ((), ())), preferred_element_type=F32
            )
        return total

    for d in (2, 1, 3):
        ig_s[d - 1] = in_term((y + d) % NY).astype(BF16)
        send(ig_s.at[d - 1], ig_r.at[d - 1], y_peer(d), R_IG1 + d - 1)
    rs_step(3)

    arrive(val_c.at[0], R_VC)
    value = val_t[0, rows(core), :] + val_c[0].astype(F32)
    for j in range(3):
        arrive(val_xr.at[j], R_VX + j)
        value = value + val_xr[j].astype(F32)
    value = value.astype(BF16).astype(F32)
    gated = (k_v[...].astype(F32) * value).astype(BF16)
    g_v[...] = gated
    send(g_v, gp_v, ctx_peer(1), R_G)
    kg_v[...] = (gg_v[...] * value).astype(BF16)
    outs = [local(kg_v, kg_hbm)]
    own = forward(gated)
    rs_step(4)
    ig_own = in_term(y)
    arrive(gp_v, R_G)
    before = forward(jnp.where(ctx == 0, jnp.zeros_like(gated), gp_v[...]))
    er = own[:BLK] - sign * before[BLK:]
    ei = own[BLK:] + sign * before[:BLK]
    hr, hi = hs_v[:BLK], hs_v[BLK:]
    filter_part = inverse(hr * er + hi * ei, hi * er - hr * ei)

    quarter = [filter_part[:, i * 128 : (i + 1) * 128] for i in range(4)]
    for i in range(4):
        fg_v[:, i * 128 : (i + 1) * 128] = quarter[i]
        fq_s[i] = quarter[i].astype(BF16)
    group = ((1, 1), (2, 4), (3, 5))
    for place, d in group:
        xh_d, core_d = (xh + d // 4) % 2, (core + d % 2) % 2
        send(fq_s.at[xh_d * 2 + core_d], fq_r.at[place - 1], plane(d), R_F1 + place - 1)
    fr, fi = fs_v[:BLK], fs_v[BLK:]
    filtered = inverse(fr * er - fi * ei, fr * ei + fi * er)
    qg_v[...] = (o_v[...].astype(F32) * filtered).astype(BF16)
    outs.append(local(qg_v, qg_hbm))
    rs_step(5)

    total = fg_v[:, pl.ds(pl.multiple_of(tb * 128, 128), 128)]
    for place in range(3):
        arrive(fq_r.at[place], R_F1 + place)
        total = total + fq_r[place].astype(F32)
    fg_v[:, :128] = total
    for i in range(NZ):
        fz_s[i] = total[i * 16 : (i + 1) * 16].astype(BF16)
    for d in range(1, NZ):
        send(fz_s.at[(z + d) % NZ], fz_r.at[d - 1], z_peer(d), R_F2 + d - 1)

    for d in range(1, NY):
        arrive(ig_r.at[d - 1], R_IG1 + d - 1)
        ig_own = ig_own + ig_r[d - 1].astype(F32)
    ig_sum[...] = ig_own.astype(BF16)
    for a in range(2):
        for b in range(2):
            xh_d, core_d = (xh + a) % 2, (core + b) % 2
            for b9 in range(2):
                src = ig_sum.at[rows(xh_d * 2 + core_d), b9 * 128 : (b9 + 1) * 128]
                dst = ig_hbm.at[:, in_slab(b9, xl, core)]
                recv = R_IG2 + (xl * 2 + core) * 2 + b9
                if a == 0 and b == 0:
                    far = pltpu.make_async_remote_copy(
                        src_ref=src, dst_ref=dst, send_sem=ssem.at[N_SEND - 3 - b9], recv_sem=rsem.at[recv],
                        device_id=dev(xh_d, xh, y, z, core_d), device_id_type=MESH,
                    )
                    near = pltpu.make_async_copy(src, dst, rsem.at[recv])

                    @pl.when(xh != xl)
                    def _():
                        far.start()

                    @pl.when(xh == xl)
                    def _():
                        near.start()

                    self_sends.append(far)
                else:
                    send(src, dst, dev(xh_d, xh, y, z, core_d), recv)

    rs_step(6)

    piece = fg_v[rows(z, 16), :128]
    for d in range(1, NZ):
        arrive(fz_r.at[d - 1], R_F2 + d - 1)
        piece = piece + fz_r[d - 1].astype(F32)
    fz_all[z] = piece.astype(BF16)
    for d in range(1, NZ):
        send(fz_all.at[z], fz_all.at[z], z_peer(d), R_F3 + d - 1)

    def w_total(half, first, second):
        arrive(rs_in.at[0, first], R_RS + first)
        arrive(rs_in.at[1, second], R_RS + 7 + second)
        total = w_term(z, half) + rs_in[0, first].astype(F32) + rs_in[1, second].astype(F32)
        return total.astype(BF16)

    wg_par[...] = w_total(xo, 5, 6)
    send(wg_par, wg_hbm.at[rows(xl), :], partner, R_WG)
    wg_own[...] = w_total(xl, 6, 5)
    outs.append(local(wg_own, wg_hbm.at[rows(xl), :]))

    for d in range(1, NZ):
        arrive(fz_all.at[(z - d + NZ) % NZ], R_F3 + d - 1)
    for i in range(NZ):
        fq_all[tb, i * 16 : (i + 1) * 16, :] = fz_all[i]
    for place, d in group:
        send(fq_all.at[tb], fq_all.at[tb], plane(d), R_F4 + place - 1)
    for place, d in group:
        xh_s, core_s = (xh + d // 4) % 2, (core + d % 2) % 2
        arrive(fq_all.at[xh_s * 2 + core_s], R_F4 + place - 1)
    for i in range(4):
        fg_v[:, i * 128 : (i + 1) * 128] = fq_all[i].astype(F32)
    outs.append(local(fg_v, fg_hbm))

    for xl_s in range(2):
        for core_s in range(2):
            for b9 in range(2):
                arrive(ig_hbm.at[:, in_slab(b9, xl_s, core_s)], R_IG2 + (xl_s * 2 + core_s) * 2 + b9)
    arrive(wg_hbm.at[rows(xo), :], R_WG)
    for copy in started:
        copy.wait_send()

    @pl.when(xh != xl)
    def _():
        for copy in self_sends:
            copy.wait_send()

    for copy in outs:
        copy.wait()


def body(inputs, w_value, q_field, k_field, filters, out_grad):
    forward, inverse = transforms()
    blk = (BLK, CH)
    vmem = pltpu.VMEM
    scratch = [
        vmem(blk, BF16), vmem(blk, BF16), vmem(blk, BF16), vmem(blk, F32),
        vmem((512, BLK), BF16), vmem((256, 256), BF16),
        vmem(blk, BF16), vmem(blk, BF16), vmem(blk, BF16), vmem(blk, BF16),
        vmem((256, CH), F32), vmem((256, CH), F32), vmem(blk, F32),
        vmem((512, 1024), BF16), vmem((2, 1024, CH), BF16), vmem((2, 512, CH), BF16),
        vmem((2, 7) + blk, BF16), vmem((2, 7) + blk, BF16),
        vmem((4, 256, CH), F32), vmem((4,) + blk, BF16), vmem((4,) + blk, BF16),
        vmem((3,) + blk, BF16), vmem((3,) + blk, BF16),
        vmem((3, 512, 256), BF16), vmem((3, 512, 256), BF16), vmem((512, 256), BF16),
        vmem(blk, BF16), vmem(blk, BF16),
        vmem((4, BLK, 128), BF16), vmem((3, BLK, 128), BF16),
        vmem((NZ, 16, 128), BF16), vmem((NZ - 1, 16, 128), BF16), vmem((NZ, 16, 128), BF16),
        vmem((4, BLK, 128), BF16), vmem(blk, F32),
        vmem(blk, BF16), vmem(blk, BF16),
        pltpu.SemaphoreType.DMA((N_SEND,)),
        pltpu.SemaphoreType.DMA((N_RECV,)),
        pltpu.SemaphoreType.DMA((N_LOCAL,)),
    ]
    any_space = pl.BlockSpec(memory_space=pl.ANY)
    return pl.pallas_call(
        kernel,
        out_shape=(
            jax.ShapeDtypeStruct((BLK, 1024), BF16),
            jax.ShapeDtypeStruct((256, CH), BF16),
            jax.ShapeDtypeStruct(blk, BF16),
            jax.ShapeDtypeStruct(blk, BF16),
            jax.ShapeDtypeStruct(blk, F32),
        ),
        in_specs=[any_space] * 8,
        out_specs=[any_space] * 5,
        scratch_shapes=scratch,
        compiler_params=pltpu.CompilerParams(
            collective_id=0, has_side_effects=True, vmem_limit_bytes=48 * 1024 * 1024
        ),
        cost_estimate=pl.CostEstimate(flops=4 * 2**30, bytes_accessed=4 * 2**20, transcendentals=0),
    )(inputs, w_value, q_field, k_field, filters, out_grad, jnp.asarray(forward), jnp.asarray(inverse))


def solution(mesh):
    return jax.shard_map(
        body,
        mesh=mesh,
        in_specs=(
            P("ctx", "chan"),
            P("ctx", "chan"),
            P("ctx", "chan"),
            P("ctx", "chan"),
            P(None, "chan"),
            P("ctx", "chan"),
        ),
        out_specs=(
            P("ctx", "chan"),
            P("ctx", "chan"),
            P("ctx", "chan"),
            P("ctx", "chan"),
            P(None, "chan"),
        ),
        check_vma=False,
    )
```

```python
import jax
import jax.numpy as jnp
import ml_dtypes
import numpy as np
from jax import lax
from jax.experimental import pallas as pl
from jax.experimental.pallas import tpu as pltpu
from jax.sharding import PartitionSpec as P

MESH = pl.DeviceIdType.MESH
F32, BF16 = jnp.float32, jnp.bfloat16
BLK = 128
CH = 512
NX, NY, NZ = 2, 4, 8
N_CTX = 2 * NZ * 2

R_IN1, R_IN2, R_WX, R_WRO, R_WRP, R_WLO, R_WLP = 0, 8, 14, 15, 19, 22, 25
R_H, R_G, R_V, R_VC, R_VX = 29, 30, 31, 38, 42
R_RS, R_RSX, R_WG, R_IG1, R_IG2 = 45, 59, 61, 62, 68
R_F1, R_F2, R_F3, R_F4 = 76, 79, 86, 93
N_RECV = 96
N_SEND = 120
N_LOCAL = 16
VMEM_LIMIT = 60 * 1024 * 1024


def transforms():
    k, n = np.arange(BLK)[:, None], np.arange(BLK)[None, :]
    angle = np.pi * (2 * k + 1) * n / (2 * BLK)
    full = np.concatenate([np.cos(angle), -np.sin(angle)], 0)
    high = full.astype(ml_dtypes.bfloat16)
    low = (full - high.astype(np.float64)).astype(ml_dtypes.bfloat16)
    forward = np.concatenate([high, low], 0)
    inverse = np.concatenate([high.T, low.T], 0).astype(np.float32) / BLK
    halves = np.concatenate([inverse[:, :BLK], inverse[:, BLK:]], 0)
    return forward, halves.astype(ml_dtypes.bfloat16)


def kernel(
    x_hbm, w_hbm, q_hbm, k_hbm, f_hbm, o_hbm, fwd_hbm, inv_hbm,
    ig_hbm, wg_hbm, qg_hbm, kg_hbm, fg_hbm,
    q_v, k_v, o_v, f_v, fwd_v, inv_v,
    h_v, hn_v, g_v, gp_v, fs_v, hs_v, gg_v,
    gin, wfull, vfull,
    rs_out, rs_in, rs_x, wx_s, wx_r,
    val_t, val_s, val_c, val_xs, val_xr,
    ig_s, ig_r, ig_sum,
    qg_v, kg_v, fq_s, fq_r, fz_s, fz_r, fz_all, fq_all, fg_v,
    wg_v,
    ssem, rsem, lsem,
):
    chan, ctx = lax.axis_index("chan"), lax.axis_index("ctx")
    xl, y = chan // NY, chan % NY
    xh, z, core = ctx // (2 * NZ), (ctx // 2) % NZ, ctx % 2
    tb = xh * 2 + core
    xo = 1 - xl

    def dev(xh_, xl_, y_, z_, core_):
        return (xl_ * NY + y_, xh_ * (2 * NZ) + z_ * 2 + core_)

    def bits(d):
        return (xh + d // 4) % 2, (xl + (d // 2) % 2) % 2, (core + d % 2) % 2

    def plane(d):
        xh_, xl_, core_ = bits(d)
        return dev(xh_, xl_, y, z, core_)

    def y_peer(d):
        return dev(xh, xl, (y + d) % NY, z, core)

    def z_peer(d):
        return dev(xh, xl, y, (z + d + NZ) % NZ, core)

    def z_partner(d):
        return dev(xh, xo, y, (z + d + NZ) % NZ, core)

    def ctx_peer(d):
        return (chan, (ctx + d + N_CTX) % N_CTX)

    right, left, partner, sibling = z_peer(1), z_peer(-1), plane(2), plane(1)
    started = []
    local_ids = iter(range(N_LOCAL))

    def send(src, dst, device, recv):
        copy = pltpu.make_async_remote_copy(
            src_ref=src, dst_ref=dst, send_sem=ssem.at[len(started)], recv_sem=rsem.at[recv],
            device_id=device, device_id_type=MESH,
        )
        copy.start()
        started.append(copy)

    def arrive(dst, recv):
        pltpu.make_async_copy(dst, dst, rsem.at[recv]).wait()

    def local(src, dst):
        copy = pltpu.make_async_copy(src, dst, lsem.at[next(local_ids)])
        copy.start()
        return copy

    def rows(index, size=BLK):
        return pl.ds(pl.multiple_of(index * size, size), size)

    def lanes(index, size=128):
        return pl.ds(pl.multiple_of(index * size, size), size)

    def dot(a, b):
        return jnp.dot(a, b, preferred_element_type=F32)

    def forward(block):
        t = dot(fwd_v[...], block)
        return t[:256] + t[256:]

    def inverse(re, im):
        spec = jnp.concatenate([re, im], 0)
        high = spec.astype(BF16)
        low = (spec - high.astype(F32)).astype(BF16)
        t = dot(inv_v[...], high)
        return t[:BLK] + t[BLK:] + dot(inv_v[:BLK], low)

    sign = (1 - 2 * (lax.broadcasted_iota(jnp.int32, (BLK, CH), 0) % 2)).astype(F32)

    loads = [local(a, b) for a, b in (
        (o_hbm, o_v), (q_hbm, q_v), (fwd_hbm, fwd_v), (f_hbm, f_v), (k_hbm, k_v),
        (inv_hbm.at[:256], inv_v.at[:, :BLK]), (inv_hbm.at[256:], inv_v.at[:, BLK:]))]
    w_local = local(w_hbm.at[rows(xl), :], wfull.at[xl, rows(z), :])
    barrier = pltpu.get_barrier_semaphore()
    greeted = [plane(d) for d in range(1, 8)] + [y_peer(d) for d in range(1, NY)]
    greeted += [z_peer(d) for d in range(1, NZ)] + [ctx_peer(1), ctx_peer(-1), z_partner(1), z_partner(-1)]
    for device in greeted:
        pl.semaphore_signal(barrier, inc=1, device_id=device, device_id_type=MESH)
    loads[0].wait()
    loads[1].wait()
    h = (o_v[...].astype(F32) * q_v[...].astype(F32)).astype(BF16)
    h_v[...] = h
    loads[2].wait()
    loads[3].wait()
    taps = f_v[...]
    taps_high = taps.astype(BF16)
    taps_low = (taps - taps_high.astype(F32)).astype(BF16)
    fs_v[...] = forward(taps_high) + dot(fwd_v[:256], taps_low)
    hs_v[...] = forward(h)
    pl.semaphore_wait(barrier, len(greeted))

    def w_piece(half, zz):
        return wfull.at[half, rows(zz), :]

    send(w_hbm.at[rows(xl), :], w_piece(xl, z), right, R_WRO)
    send(w_hbm.at[rows(xl), :], w_piece(xl, z), left, R_WLO)
    send(w_hbm.at[rows(xo), :], w_piece(xl, z), partner, R_WX)
    send(h_v, hn_v, ctx_peer(-1), R_H)

    def in_slab(b9, xl_, core_):
        return lanes(b9 * 4 + core_ * 2 + xl_)

    def gin_slab(place, b9):
        return gin.at[rows(place), lanes(y * 2 + b9)]

    self_sends = []

    def send_or_copy(src, dst, device, recv, same_x):
        if not same_x:
            return send(src, dst, device, recv)
        far = pltpu.make_async_remote_copy(
            src_ref=src, dst_ref=dst, send_sem=ssem.at[N_SEND - 1 - len(self_sends)], recv_sem=rsem.at[recv],
            device_id=device, device_id_type=MESH,
        )
        near = pltpu.make_async_copy(src, dst, rsem.at[recv])
        self_sends.append(far)

        @pl.when(xh != xl)
        def _():
            far.start()

        @pl.when(xh == xl)
        def _():
            near.start()

    for a in (1, 0):
        for b in (1, 0):
            xl_d, core_d = (xl + a) % 2, (core + b) % 2
            for b9 in range(2):
                src = x_hbm.at[:, in_slab(b9, xl_d, core_d)]
                send_or_copy(src, gin_slab(tb, b9), dev(xl, xl_d, y, z, core_d), R_IN1 + tb * 2 + b9, a + b == 0)

    def gin_part(place, yy):
        return gin.at[rows(place, 256), lanes(yy, 256)]

    def in_second(turn):
        place = (xl + turn) % 2
        for i in range(2):
            for b9 in range(2):
                arrive(gin_slab(place * 2 + i, b9), R_IN1 + (place * 2 + i) * 2 + b9)
        for d in (2, 1, 3):
            send(gin_part(place, y), gin_part(place, y), y_peer(d), R_IN2 + (d - 1) * 2 + place)

    def w_own(k):
        piece = w_piece(xl, (z - k + NZ) % NZ)
        arrive(piece, R_WRO + k - 1)
        if k < 4:
            send(piece, piece, right, R_WRO + k)
            piece = w_piece(xl, (z + k) % NZ)
            arrive(piece, R_WLO + k - 1)
            if k < 3:
                send(piece, piece, left, R_WLO + k)

    def w_par(k):
        piece = w_piece(xo, (z + k) % NZ)
        arrive(piece, R_WLP + k - 1)
        if k < 4:
            send(piece, piece, left, R_WLP + k)
            piece = w_piece(xo, (z - k + NZ) % NZ)
            arrive(piece, R_WRP + k - 1)
            if k < 3:
                send(piece, piece, right, R_WRP + k)

    w_local.wait()
    w_own(1)
    arrive(w_piece(xo, z), R_WX)
    send(w_piece(xo, z), w_piece(xo, z), left, R_WLP)
    send(w_piece(xo, z), w_piece(xo, z), right, R_WRP)
    in_second(0)

    arrive(hn_v, R_H)
    for load in loads[4:]:
        load.wait()
    hn = forward(jnp.where(ctx == N_CTX - 1, jnp.zeros_like(h), hn_v[...]))
    hr = hs_v[:BLK] + sign * hn[BLK:]
    hi = hs_v[BLK:] - sign * hn[:BLK]
    hs_v[:BLK] = hr
    hs_v[BLK:] = hi
    fr, fi = fs_v[:BLK], fs_v[BLK:]
    g_grad = inverse(fr * hr + fi * hi, fr * hi - fi * hr)
    gg_v[...] = g_grad
    vfull[xl, rows(tb), :] = (g_grad * k_v[...].astype(F32)).astype(BF16)

    def v_piece(d):
        xh_, xl_, core_ = bits(d)
        return vfull.at[xl_, rows(xh_ * 2 + core_), :]

    for d in (4, 6, 2, 1):
        send(v_piece(0), v_piece(0), plane(d), R_V + d - 1)
    in_second(1)
    w_own(2)
    w_par(1)
    w_own(3)
    w_par(2)
    for d in (2, 6, 4):
        arrive(v_piece(d), R_V + d - 1)
        send(v_piece(d), v_piece(d), sibling, R_V + d)
    w_own(4)
    w_par(3)
    for d in (1, 3, 5, 7):
        arrive(v_piece(d), R_V + d - 1)
    for place in range(2):
        for d in range(1, NY):
            arrive(gin_part(place, (y - d + NY) % NY), R_IN2 + (d - 1) * 2 + place)

    def w_term(zz, half):
        return lax.dot_general(
            gin[:, lanes(zz)], vfull[half], (((0,), (0,)), ((), ())), preferred_element_type=F32
        )

    def rs_step(i):
        hop = 4 - (i + 1) // 2
        for way, step in ((0, 1), (1, -1)):
            own = (i + way) % 2 == 0
            term = w_term((z + step * hop + NZ) % NZ, xl if own else xo)
            if i >= 2:
                arrive(rs_in.at[way, i - 2], R_RS + way * 7 + i - 2)
                term = term + rs_in[way, i - 2].astype(F32)
            rs_out[way, i] = term.astype(BF16)
            if hop == 1 and not own:
                send(rs_out.at[way, i], rs_x.at[way], z_partner(step), R_RSX + way)
            else:
                send(rs_out.at[way, i], rs_in.at[way, i], z_peer(step), R_RS + way * 7 + i)

    rs_step(0)
    rs_step(1)

    def val_part(j):
        xh_d, xl_d, _ = bits(2 * j)
        val_t[j] = dot(gin[rows(xh_d, 256), :], wfull[xl_d])
        val_s[j] = val_t[j, rows(1 - core), :].astype(BF16)
        send(val_s.at[j], val_c.at[j], sibling, R_VC + j)

    def val_send(j):
        arrive(val_c.at[j], R_VC + j)
        val_xs[j - 1] = (val_t[j, rows(core), :] + val_c[j].astype(F32)).astype(BF16)
        send(val_xs.at[j - 1], val_xr.at[j - 1], plane(2 * j), R_VX + j - 1)

    val_part(2)
    val_part(0)
    val_send(2)
    w_par(4)
    val_part(1)
    val_part(3)
    val_send(1)
    val_send(3)
    rs_step(2)

    def in_term(place, yy):
        total = 0.0
        for half in range(2):
            total = total + lax.dot_general(
                vfull[half, rows(place, 256), :], wfull[half, rows(yy, 256), :], (((1,), (1,)), ((), ())),
                preferred_element_type=F32,
            )
        return total

    def ig_first(turn):
        place = (xo + turn) % 2
        for d in (2, 1, 3):
            slot = (d - 1) * 2 + turn
            ig_s[slot] = in_term(place, (y + d) % NY).astype(BF16)
            send(ig_s.at[slot], ig_r.at[slot], y_peer(d), R_IG1 + slot)

    def ig_second(turn):
        place = (xo + turn) % 2
        total = in_term(place, y)
        for d in (1, 3, 2):
            slot = (d - 1) * 2 + turn
            arrive(ig_r.at[slot], R_IG1 + slot)
            total = total + ig_r[slot].astype(F32)
        ig_sum[turn] = total.astype(BF16)
        for b in (1, 0):
            core_d = (core + b) % 2
            for b9 in range(2):
                src = ig_sum.at[turn, rows(core_d), b9 * 128 : (b9 + 1) * 128]
                dst = ig_hbm.at[:, in_slab(b9, xl, core)]
                send_or_copy(src, dst, dev(place, xh, y, z, core_d), R_IG2 + (xl * 2 + core) * 2 + b9, turn + b == 1 and b == 0)

    ig_first(0)
    ig_first(1)
    rs_step(3)
    wx_s[...] = w_term(z, xo).astype(BF16)
    send(wx_s, wx_r, partner, R_WG)

    arrive(val_c.at[0], R_VC)
    value = val_t[0, rows(core), :] + val_c[0].astype(F32)
    for j in (2, 1, 3):
        arrive(val_xr.at[j - 1], R_VX + j - 1)
        value = value + val_xr[j - 1].astype(F32)
    value = value.astype(BF16).astype(F32)
    gated = (k_v[...].astype(F32) * value).astype(BF16)
    g_v[...] = gated
    send(g_v, gp_v, ctx_peer(1), R_G)
    own = forward(gated)
    hr, hi = hs_v[:BLK], hs_v[BLK:]
    filter_part = inverse(own[:BLK] * hr + own[BLK:] * hi, own[:BLK] * hi - own[BLK:] * hr)
    fg_v[...] = filter_part

    for i in range(4):
        fq_s[i] = filter_part[:, i * 128 : (i + 1) * 128].astype(BF16)
    group = ((1, 1), (2, 4), (3, 5))
    for place, d in group:
        xh_d, _, core_d = bits(d)
        send(fq_s.at[xh_d * 2 + core_d], fq_r.at[place - 1], plane(d), R_F1 + place - 1)
    kg_v[...] = (gg_v[...] * value).astype(BF16)
    outs = [local(kg_v, kg_hbm)]
    rs_step(4)

    total = fg_v[:, lanes(tb)]
    for place in range(3):
        arrive(fq_r.at[place], R_F1 + place)
        total = total + fq_r[place].astype(F32)
    fg_v[:, :128] = total
    for i in range(NZ):
        fz_s[i] = total[i * 16 : (i + 1) * 16].astype(BF16)
    for d in range(1, NZ):
        send(fz_s.at[(z + d) % NZ], fz_r.at[d - 1], z_peer(d), R_F2 + d - 1)
    rs_step(5)
    ig_second(0)

    arrive(gp_v, R_G)
    before = forward(jnp.where(ctx == 0, jnp.zeros_like(gated), gp_v[...]))
    er = own[:BLK] - sign * before[BLK:]
    ei = own[BLK:] + sign * before[:BLK]
    fr, fi = fs_v[:BLK], fs_v[BLK:]
    filtered = inverse(fr * er - fi * ei, fr * ei + fi * er)
    qg_v[...] = (o_v[...].astype(F32) * filtered).astype(BF16)
    outs.append(local(qg_v, qg_hbm))

    piece = fg_v[rows(z, 16), :128]
    for d in range(1, NZ):
        arrive(fz_r.at[d - 1], R_F2 + d - 1)
        piece = piece + fz_r[d - 1].astype(F32)
    fz_all[z] = piece.astype(BF16)
    for d in range(1, NZ):
        send(fz_all.at[z], fz_all.at[z], z_peer(d), R_F3 + d - 1)
    rs_step(6)
    ig_second(1)

    for d in range(1, NZ):
        arrive(fz_all.at[(z - d + NZ) % NZ], R_F3 + d - 1)
    for i in range(NZ):
        fq_all[tb, i * 16 : (i + 1) * 16, :] = fz_all[i]
    for place, d in group:
        send(fq_all.at[tb], fq_all.at[tb], plane(d), R_F4 + place - 1)

    term = w_term(z, xl)
    arrive(rs_in.at[1, 5], R_RS + 7 + 5)
    term = term + rs_in[1, 5].astype(F32)
    arrive(wx_r, R_WG)
    arrive(rs_x.at[0], R_RSX)
    other = wx_r[...].astype(F32) + rs_x[0].astype(F32)
    arrive(rs_in.at[0, 6], R_RS + 6)
    wg_v[0] = (term + rs_in[0, 6].astype(F32)).astype(BF16)
    outs.append(local(wg_v.at[0], wg_hbm.at[rows(xl), :]))
    arrive(rs_x.at[1], R_RSX + 1)
    wg_v[1] = (other + rs_x[1].astype(F32)).astype(BF16)
    outs.append(local(wg_v.at[1], wg_hbm.at[rows(xo), :]))

    for place, d in group:
        xh_s, _, core_s = bits(d)
        arrive(fq_all.at[xh_s * 2 + core_s], R_F4 + place - 1)
    for i in range(4):
        fg_v[:, i * 128 : (i + 1) * 128] = fq_all[i].astype(F32)
    outs.append(local(fg_v, fg_hbm))

    for xl_s in range(2):
        for core_s in range(2):
            for b9 in range(2):
                arrive(ig_hbm.at[:, in_slab(b9, xl_s, core_s)], R_IG2 + (xl_s * 2 + core_s) * 2 + b9)
    for copy in started:
        copy.wait_send()

    @pl.when(xh != xl)
    def _():
        for copy in self_sends:
            copy.wait_send()

    for copy in outs:
        copy.wait()


def copy_kernel(*refs):
    sources, targets, sem = refs[:5], refs[5:10], refs[10]
    copies = [pltpu.make_async_copy(a, b, sem.at[i]) for i, (a, b) in enumerate(zip(sources, targets))]
    for copy in copies:
        copy.start()
    for copy in copies:
        copy.wait()


def body(inputs, w_value, q_field, k_field, filters, out_grad):
    forward, inverse = transforms()
    blk = (BLK, CH)
    vmem = pltpu.VMEM
    scratch = [
        vmem(blk, BF16), vmem(blk, BF16), vmem(blk, BF16), vmem(blk, F32),
        vmem((512, BLK), BF16), vmem((256, 256), BF16),
        vmem(blk, BF16), vmem(blk, BF16), vmem(blk, BF16), vmem(blk, BF16),
        vmem((256, CH), F32), vmem((256, CH), F32), vmem(blk, F32),
        vmem((512, 1024), BF16), vmem((2, 1024, CH), BF16), vmem((2, 512, CH), BF16),
        vmem((2, 7) + blk, BF16), vmem((2, 7) + blk, BF16), vmem((2,) + blk, BF16),
        vmem(blk, BF16), vmem(blk, BF16),
        vmem((4, 256, CH), F32), vmem((4,) + blk, BF16), vmem((4,) + blk, BF16),
        vmem((3,) + blk, BF16), vmem((3,) + blk, BF16),
        vmem((6, 256, 256), BF16), vmem((6, 256, 256), BF16), vmem((2, 256, 256), BF16),
        vmem(blk, BF16), vmem(blk, BF16),
        vmem((4, BLK, 128), BF16), vmem((3, BLK, 128), BF16),
        vmem((NZ, 16, 128), BF16), vmem((NZ - 1, 16, 128), BF16), vmem((NZ, 16, 128), BF16),
        vmem((4, BLK, 128), BF16), vmem(blk, F32),
        vmem((2,) + blk, BF16),
        pltpu.SemaphoreType.DMA((N_SEND,)),
        pltpu.SemaphoreType.DMA((N_RECV,)),
        pltpu.SemaphoreType.DMA((N_LOCAL,)),
    ]
    any_space = pl.BlockSpec(memory_space=pl.ANY)
    hbm_space = pl.BlockSpec(memory_space=pltpu.HBM)
    shapes = (
        jax.ShapeDtypeStruct((BLK, 1024), BF16),
        jax.ShapeDtypeStruct((256, CH), BF16),
        jax.ShapeDtypeStruct(blk, BF16),
        jax.ShapeDtypeStruct(blk, BF16),
        jax.ShapeDtypeStruct(blk, F32),
    )
    results = pl.pallas_call(
        kernel,
        out_shape=tuple(vmem(s.shape, s.dtype) for s in shapes),
        in_specs=[hbm_space] * 8,
        out_specs=[any_space] * 5,
        scratch_shapes=scratch,
        compiler_params=pltpu.CompilerParams(
            collective_id=0, has_side_effects=True, vmem_limit_bytes=VMEM_LIMIT
        ),
        cost_estimate=pl.CostEstimate(flops=4 * 2**30, bytes_accessed=4 * 2**20, transcendentals=0),
    )(inputs, w_value, q_field, k_field, filters, out_grad, jnp.asarray(forward), jnp.asarray(inverse))
    return pl.pallas_call(
        copy_kernel,
        out_shape=shapes,
        in_specs=[any_space] * 5,
        out_specs=[hbm_space] * 5,
        scratch_shapes=[pltpu.SemaphoreType.DMA((5,))],
        compiler_params=pltpu.CompilerParams(vmem_limit_bytes=8 * 1024 * 1024),
    )(*results)


def solution(mesh):
    return jax.shard_map(
        body,
        mesh=mesh,
        in_specs=(
            P("ctx", "chan"),
            P("ctx", "chan"),
            P("ctx", "chan"),
            P("ctx", "chan"),
            P(None, "chan"),
            P("ctx", "chan"),
        ),
        out_specs=(
            P("ctx", "chan"),
            P("ctx", "chan"),
            P("ctx", "chan"),
            P("ctx", "chan"),
            P(None, "chan"),
        ),
        check_vma=False,
    )
```

```python
import jax
import jax.numpy as jnp
import ml_dtypes
import numpy as np
from jax import lax
from jax.experimental import pallas as pl
from jax.experimental.pallas import tpu as pltpu
from jax.sharding import PartitionSpec as P

MESH = pl.DeviceIdType.MESH
F32, BF16 = jnp.float32, jnp.bfloat16
BLK = 128
CH = 512
NX, NY, NZ = 2, 4, 8
N_CTX = 2 * NZ * 2

R_IN1, R_IN2, R_WX, R_WR, R_WL = 0, 8, 14, 16, 32
R_H, R_G, R_V, R_VC, R_VX = 48, 49, 50, 57, 61
R_RS, R_RSX, R_WG, R_IG1, R_IG2 = 64, 78, 80, 81, 87
R_F1, R_F2, R_F3, R_F4 = 95, 98, 105, 112
N_RECV = 115
N_SEND = 140
N_LOCAL = 16
VMEM_LIMIT = 60 * 1024 * 1024


def transforms():
    k, n = np.arange(BLK)[:, None], np.arange(BLK)[None, :]
    angle = np.pi * (2 * k + 1) * n / (2 * BLK)
    full = np.concatenate([np.cos(angle), -np.sin(angle)], 0)
    high = full.astype(ml_dtypes.bfloat16)
    low = (full - high.astype(np.float64)).astype(ml_dtypes.bfloat16)
    forward = np.concatenate([high, low], 0)
    inverse = np.concatenate([high.T, low.T], 0).astype(np.float32) / BLK
    halves = np.concatenate([inverse[:, :BLK], inverse[:, BLK:]], 0)
    return forward, halves.astype(ml_dtypes.bfloat16)


def kernel(
    x_hbm, w_hbm, q_hbm, k_hbm, f_hbm, o_hbm, fwd_hbm, inv_hbm,
    ig_hbm, wg_hbm, qg_hbm, kg_hbm, fg_hbm,
    q_v, k_v, o_v, f_v, fwd_v, inv_v,
    h_v, hn_v, g_v, gp_v, fs_v, hs_v, gg_v,
    gin, wfull, vfull,
    rs_out, rs_in, rs_x, wx_s, wx_r,
    val_t, val_s, val_c, val_xs, val_xr,
    ig_s, ig_r, ig_sum,
    qg_v, kg_v, fq_s, fq_r, fz_s, fz_r, fz_all, fq_all, fg_v,
    wg_v,
    ssem, rsem, lsem,
):
    chan, ctx = lax.axis_index("chan"), lax.axis_index("ctx")
    xl, y = chan // NY, chan % NY
    xh, z, core = ctx // (2 * NZ), (ctx // 2) % NZ, ctx % 2
    tb = xh * 2 + core
    xo = 1 - xl

    def dev(xh_, xl_, y_, z_, core_):
        return (xl_ * NY + y_, xh_ * (2 * NZ) + z_ * 2 + core_)

    def bits(d):
        return (xh + d // 4) % 2, (xl + (d // 2) % 2) % 2, (core + d % 2) % 2

    def plane(d):
        xh_, xl_, core_ = bits(d)
        return dev(xh_, xl_, y, z, core_)

    def y_peer(d):
        return dev(xh, xl, (y + d) % NY, z, core)

    def z_peer(d):
        return dev(xh, xl, y, (z + d + NZ) % NZ, core)

    def z_partner(d):
        return dev(xh, xo, y, (z + d + NZ) % NZ, core)

    def ctx_peer(d):
        return (chan, (ctx + d + N_CTX) % N_CTX)

    right, left, partner, sibling = z_peer(1), z_peer(-1), plane(2), plane(1)
    started = []
    local_ids = iter(range(N_LOCAL))

    def send(src, dst, device, recv):
        copy = pltpu.make_async_remote_copy(
            src_ref=src, dst_ref=dst, send_sem=ssem.at[len(started)], recv_sem=rsem.at[recv],
            device_id=device, device_id_type=MESH,
        )
        copy.start()
        started.append(copy)

    def arrive(dst, recv):
        pltpu.make_async_copy(dst, dst, rsem.at[recv]).wait()

    def local(src, dst):
        copy = pltpu.make_async_copy(src, dst, lsem.at[next(local_ids)])
        copy.start()
        return copy

    def rows(index, size=BLK):
        return pl.ds(pl.multiple_of(index * size, size), size)

    def lanes(index, size=128):
        return pl.ds(pl.multiple_of(index * size, size), size)

    def dot(a, b):
        return jnp.dot(a, b, preferred_element_type=F32)

    def forward(block):
        t = dot(fwd_v[...], block)
        return t[:256] + t[256:]

    def inverse(re, im):
        spec = jnp.concatenate([re, im], 0)
        high = spec.astype(BF16)
        low = (spec - high.astype(F32)).astype(BF16)
        t = dot(inv_v[...], high)
        return t[:BLK] + t[BLK:] + dot(inv_v[:BLK], low)

    sign = (1 - 2 * (lax.broadcasted_iota(jnp.int32, (BLK, CH), 0) % 2)).astype(F32)

    loads = [local(a, b) for a, b in (
        (o_hbm, o_v), (q_hbm, q_v), (fwd_hbm, fwd_v), (f_hbm, f_v), (k_hbm, k_v),
        (inv_hbm.at[:256], inv_v.at[:, :BLK]), (inv_hbm.at[256:], inv_v.at[:, BLK:]))]
    w_local = local(w_hbm.at[rows(xl), :], wfull.at[xl, rows(z), :])
    barrier = pltpu.get_barrier_semaphore()
    greeted = [plane(d) for d in range(1, 8)] + [y_peer(d) for d in range(1, NY)]
    greeted += [z_peer(d) for d in range(1, NZ)] + [ctx_peer(1), ctx_peer(-1), z_partner(1), z_partner(-1)]
    for device in greeted:
        pl.semaphore_signal(barrier, inc=1, device_id=device, device_id_type=MESH)
    pl.semaphore_wait(barrier, len(greeted))

    def w_piece(stream, zz):
        return wfull.at[xl if stream < 2 else xo, rows(zz * 2 + stream % 2, 64), :]

    def w_start(stream, src):
        send(src, w_piece(stream, z), right, R_WR + stream * 4)
        send(src, w_piece(stream, z), left, R_WL + stream * 4)

    for part in range(2):
        send(w_hbm.at[rows(xo * 2 + part, 64), :], w_piece(part, z), partner, R_WX + part)
    for part in range(2):
        w_start(part, w_hbm.at[rows(xl * 2 + part, 64), :])

    def in_slab(b9, xl_, core_):
        return lanes(b9 * 4 + core_ * 2 + xl_)

    def gin_slab(place, b9):
        return gin.at[rows(place), lanes(y * 2 + b9)]

    self_sends = []

    def send_or_copy(src, dst, device, recv, same_x):
        if not same_x:
            return send(src, dst, device, recv)
        far = pltpu.make_async_remote_copy(
            src_ref=src, dst_ref=dst, send_sem=ssem.at[N_SEND - 1 - len(self_sends)], recv_sem=rsem.at[recv],
            device_id=device, device_id_type=MESH,
        )
        near = pltpu.make_async_copy(src, dst, rsem.at[recv])
        self_sends.append(far)

        @pl.when(xh != xl)
        def _():
            far.start()

        @pl.when(xh == xl)
        def _():
            near.start()

    for a in (1, 0):
        for b in (1, 0):
            xl_d, core_d = (xl + a) % 2, (core + b) % 2
            for b9 in range(2):
                src = x_hbm.at[:, in_slab(b9, xl_d, core_d)]
                send_or_copy(src, gin_slab(tb, b9), dev(xl, xl_d, y, z, core_d), R_IN1 + tb * 2 + b9, a + b == 0)

    loads[0].wait()
    loads[1].wait()
    h = (o_v[...].astype(F32) * q_v[...].astype(F32)).astype(BF16)
    h_v[...] = h
    send(h_v, hn_v, ctx_peer(-1), R_H)
    loads[2].wait()
    loads[3].wait()
    taps = f_v[...]
    taps_high = taps.astype(BF16)
    taps_low = (taps - taps_high.astype(F32)).astype(BF16)
    fs_v[...] = forward(taps_high) + dot(fwd_v[:256], taps_low)
    hs_v[...] = forward(h)

    def gin_part(place, yy):
        return gin.at[rows(place, 256), lanes(yy, 256)]

    def in_second(turn):
        place = (xl + turn) % 2
        for i in range(2):
            for b9 in range(2):
                arrive(gin_slab(place * 2 + i, b9), R_IN1 + (place * 2 + i) * 2 + b9)
        for d in (2, 1, 3):
            send(gin_part(place, y), gin_part(place, y), y_peer(d), R_IN2 + (d - 1) * 2 + place)

    def w_step(stream, k):
        for step, base, hops in ((1, R_WR, 4 - stream % 2), (-1, R_WL, 3 + stream % 2)):
            if k > hops:
                continue
            piece = w_piece(stream, (z - step * k + NZ) % NZ)
            arrive(piece, base + stream * 4 + k - 1)
            if k < hops:
                send(piece, piece, z_peer(step), base + stream * 4 + k)

    def w_own(k):
        w_step(0, k)
        w_step(1, k)

    def w_par(k):
        w_step(2, k)
        w_step(3, k)

    w_local.wait()
    w_own(1)
    for part in range(2):
        arrive(w_piece(2 + part, z), R_WX + part)
        w_start(2 + part, w_piece(2 + part, z))
    in_second(0)

    arrive(hn_v, R_H)
    for load in loads[4:]:
        load.wait()
    hn = forward(jnp.where(ctx == N_CTX - 1, jnp.zeros_like(h), hn_v[...]))
    hr = hs_v[:BLK] + sign * hn[BLK:]
    hi = hs_v[BLK:] - sign * hn[:BLK]
    hs_v[:BLK] = hr
    hs_v[BLK:] = hi
    fr, fi = fs_v[:BLK], fs_v[BLK:]
    g_grad = inverse(fr * hr + fi * hi, fr * hi - fi * hr)
    gg_v[...] = g_grad
    vfull[xl, rows(tb), :] = (g_grad * k_v[...].astype(F32)).astype(BF16)

    def v_piece(d):
        xh_, xl_, core_ = bits(d)
        return vfull.at[xl_, rows(xh_ * 2 + core_), :]

    for d in (4, 6, 2, 1):
        send(v_piece(0), v_piece(0), plane(d), R_V + d - 1)
    in_second(1)
    w_own(2)
    w_par(1)
    w_own(3)
    w_par(2)
    for d in (2, 6, 4):
        arrive(v_piece(d), R_V + d - 1)
        send(v_piece(d), v_piece(d), sibling, R_V + d)
    w_own(4)
    w_par(3)
    for d in (1, 3, 5, 7):
        arrive(v_piece(d), R_V + d - 1)
    for place in range(2):
        for d in range(1, NY):
            arrive(gin_part(place, (y - d + NY) % NY), R_IN2 + (d - 1) * 2 + place)

    def w_term(zz, half):
        return lax.dot_general(
            gin[:, lanes(zz)], vfull[half], (((0,), (0,)), ((), ())), preferred_element_type=F32
        )

    def rs_step(i):
        hop = 4 - (i + 1) // 2
        for way, step in ((0, 1), (1, -1)):
            own = (i + way) % 2 == 0
            term = w_term((z + step * hop + NZ) % NZ, xl if own else xo)
            if i >= 2:
                arrive(rs_in.at[way, i - 2], R_RS + way * 7 + i - 2)
                term = term + rs_in[way, i - 2].astype(F32)
            rs_out[way, i] = term.astype(BF16)
            if hop == 1 and not own:
                send(rs_out.at[way, i], rs_x.at[way], z_partner(step), R_RSX + way)
            else:
                send(rs_out.at[way, i], rs_in.at[way, i], z_peer(step), R_RS + way * 7 + i)

    rs_step(0)
    rs_step(1)

    def val_part(j):
        xh_d, xl_d, _ = bits(2 * j)
        val_t[j] = dot(gin[rows(xh_d, 256), :], wfull[xl_d])
        val_s[j] = val_t[j, rows(1 - core), :].astype(BF16)
        send(val_s.at[j], val_c.at[j], sibling, R_VC + j)

    def val_send(j):
        arrive(val_c.at[j], R_VC + j)
        val_xs[j - 1] = (val_t[j, rows(core), :] + val_c[j].astype(F32)).astype(BF16)
        send(val_xs.at[j - 1], val_xr.at[j - 1], plane(2 * j), R_VX + j - 1)

    val_part(2)
    val_part(0)
    val_send(2)
    w_par(4)
    val_part(1)
    val_part(3)
    val_send(1)
    val_send(3)
    rs_step(2)

    def in_term(place, yy):
        total = 0.0
        for half in range(2):
            total = total + lax.dot_general(
                vfull[half, rows(place, 256), :], wfull[half, rows(yy, 256), :], (((1,), (1,)), ((), ())),
                preferred_element_type=F32,
            )
        return total

    def ig_first(turn):
        place = (xo + turn) % 2
        for d in (2, 1, 3):
            slot = (d - 1) * 2 + turn
            ig_s[slot] = in_term(place, (y + d) % NY).astype(BF16)
            send(ig_s.at[slot], ig_r.at[slot], y_peer(d), R_IG1 + slot)

    def ig_second(turn):
        place = (xo + turn) % 2
        total = in_term(place, y)
        for d in (1, 3, 2):
            slot = (d - 1) * 2 + turn
            arrive(ig_r.at[slot], R_IG1 + slot)
            total = total + ig_r[slot].astype(F32)
        ig_sum[turn] = total.astype(BF16)
        for b in (1, 0):
            core_d = (core + b) % 2
            for b9 in range(2):
                src = ig_sum.at[turn, rows(core_d), b9 * 128 : (b9 + 1) * 128]
                dst = ig_hbm.at[:, in_slab(b9, xl, core)]
                send_or_copy(src, dst, dev(place, xh, y, z, core_d), R_IG2 + (xl * 2 + core) * 2 + b9, turn + b == 1 and b == 0)

    ig_first(0)
    ig_first(1)
    rs_step(3)
    wx_s[...] = w_term(z, xo).astype(BF16)
    send(wx_s, wx_r, partner, R_WG)

    arrive(val_c.at[0], R_VC)
    value = val_t[0, rows(core), :] + val_c[0].astype(F32)
    for j in (2, 1, 3):
        arrive(val_xr.at[j - 1], R_VX + j - 1)
        value = value + val_xr[j - 1].astype(F32)
    value = value.astype(BF16).astype(F32)
    gated = (k_v[...].astype(F32) * value).astype(BF16)
    g_v[...] = gated
    send(g_v, gp_v, ctx_peer(1), R_G)
    own = forward(gated)
    hr, hi = hs_v[:BLK], hs_v[BLK:]
    filter_part = inverse(own[:BLK] * hr + own[BLK:] * hi, own[:BLK] * hi - own[BLK:] * hr)
    fg_v[...] = filter_part

    for i in range(4):
        fq_s[i] = filter_part[:, i * 128 : (i + 1) * 128].astype(BF16)
    group = ((1, 1), (2, 4), (3, 5))
    for place, d in group:
        xh_d, _, core_d = bits(d)
        send(fq_s.at[xh_d * 2 + core_d], fq_r.at[place - 1], plane(d), R_F1 + place - 1)
    kg_v[...] = (gg_v[...] * value).astype(BF16)
    outs = [local(kg_v, kg_hbm)]
    rs_step(4)

    total = fg_v[:, lanes(tb)]
    for place in range(3):
        arrive(fq_r.at[place], R_F1 + place)
        total = total + fq_r[place].astype(F32)
    fg_v[:, :128] = total
    for i in range(NZ):
        fz_s[i] = total[i * 16 : (i + 1) * 16].astype(BF16)
    for d in range(1, NZ):
        send(fz_s.at[(z + d) % NZ], fz_r.at[d - 1], z_peer(d), R_F2 + d - 1)
    rs_step(5)
    ig_second(0)

    arrive(gp_v, R_G)
    before = forward(jnp.where(ctx == 0, jnp.zeros_like(gated), gp_v[...]))
    er = own[:BLK] - sign * before[BLK:]
    ei = own[BLK:] + sign * before[:BLK]
    fr, fi = fs_v[:BLK], fs_v[BLK:]
    filtered = inverse(fr * er - fi * ei, fr * ei + fi * er)
    qg_v[...] = (o_v[...].astype(F32) * filtered).astype(BF16)
    outs.append(local(qg_v, qg_hbm))

    piece = fg_v[rows(z, 16), :128]
    for d in range(1, NZ):
        arrive(fz_r.at[d - 1], R_F2 + d - 1)
        piece = piece + fz_r[d - 1].astype(F32)
    fz_all[z] = piece.astype(BF16)
    for d in range(1, NZ):
        send(fz_all.at[z], fz_all.at[z], z_peer(d), R_F3 + d - 1)
    rs_step(6)
    ig_second(1)

    for d in range(1, NZ):
        arrive(fz_all.at[(z - d + NZ) % NZ], R_F3 + d - 1)
    for i in range(NZ):
        fq_all[tb, i * 16 : (i + 1) * 16, :] = fz_all[i]
    for place, d in group:
        send(fq_all.at[tb], fq_all.at[tb], plane(d), R_F4 + place - 1)

    term = w_term(z, xl)
    arrive(rs_in.at[1, 5], R_RS + 7 + 5)
    term = term + rs_in[1, 5].astype(F32)
    arrive(wx_r, R_WG)
    arrive(rs_x.at[0], R_RSX)
    other = wx_r[...].astype(F32) + rs_x[0].astype(F32)
    arrive(rs_in.at[0, 6], R_RS + 6)
    wg_v[0] = (term + rs_in[0, 6].astype(F32)).astype(BF16)
    outs.append(local(wg_v.at[0], wg_hbm.at[rows(xl), :]))
    arrive(rs_x.at[1], R_RSX + 1)
    wg_v[1] = (other + rs_x[1].astype(F32)).astype(BF16)
    outs.append(local(wg_v.at[1], wg_hbm.at[rows(xo), :]))

    for place, d in group:
        xh_s, _, core_s = bits(d)
        arrive(fq_all.at[xh_s * 2 + core_s], R_F4 + place - 1)
    for i in range(4):
        fg_v[:, i * 128 : (i + 1) * 128] = fq_all[i].astype(F32)
    outs.append(local(fg_v, fg_hbm))

    for xl_s in range(2):
        for core_s in range(2):
            for b9 in range(2):
                arrive(ig_hbm.at[:, in_slab(b9, xl_s, core_s)], R_IG2 + (xl_s * 2 + core_s) * 2 + b9)
    for copy in started:
        copy.wait_send()

    @pl.when(xh != xl)
    def _():
        for copy in self_sends:
            copy.wait_send()

    for copy in outs:
        copy.wait()


def copy_kernel(*refs):
    sources, targets, sem = refs[:5], refs[5:10], refs[10]
    copies = [pltpu.make_async_copy(a, b, sem.at[i]) for i, (a, b) in enumerate(zip(sources, targets))]
    for copy in copies:
        copy.start()
    for copy in copies:
        copy.wait()


def body(inputs, w_value, q_field, k_field, filters, out_grad):
    forward, inverse = transforms()
    blk = (BLK, CH)
    vmem = pltpu.VMEM
    scratch = [
        vmem(blk, BF16), vmem(blk, BF16), vmem(blk, BF16), vmem(blk, F32),
        vmem((512, BLK), BF16), vmem((256, 256), BF16),
        vmem(blk, BF16), vmem(blk, BF16), vmem(blk, BF16), vmem(blk, BF16),
        vmem((256, CH), F32), vmem((256, CH), F32), vmem(blk, F32),
        vmem((512, 1024), BF16), vmem((2, 1024, CH), BF16), vmem((2, 512, CH), BF16),
        vmem((2, 7) + blk, BF16), vmem((2, 7) + blk, BF16), vmem((2,) + blk, BF16),
        vmem(blk, BF16), vmem(blk, BF16),
        vmem((4, 256, CH), F32), vmem((4,) + blk, BF16), vmem((4,) + blk, BF16),
        vmem((3,) + blk, BF16), vmem((3,) + blk, BF16),
        vmem((6, 256, 256), BF16), vmem((6, 256, 256), BF16), vmem((2, 256, 256), BF16),
        vmem(blk, BF16), vmem(blk, BF16),
        vmem((4, BLK, 128), BF16), vmem((3, BLK, 128), BF16),
        vmem((NZ, 16, 128), BF16), vmem((NZ - 1, 16, 128), BF16), vmem((NZ, 16, 128), BF16),
        vmem((4, BLK, 128), BF16), vmem(blk, F32),
        vmem((2,) + blk, BF16),
        pltpu.SemaphoreType.DMA((N_SEND,)),
        pltpu.SemaphoreType.DMA((N_RECV,)),
        pltpu.SemaphoreType.DMA((N_LOCAL,)),
    ]
    any_space = pl.BlockSpec(memory_space=pl.ANY)
    hbm_space = pl.BlockSpec(memory_space=pltpu.HBM)
    shapes = (
        jax.ShapeDtypeStruct((BLK, 1024), BF16),
        jax.ShapeDtypeStruct((256, CH), BF16),
        jax.ShapeDtypeStruct(blk, BF16),
        jax.ShapeDtypeStruct(blk, BF16),
        jax.ShapeDtypeStruct(blk, F32),
    )
    results = pl.pallas_call(
        kernel,
        out_shape=tuple(vmem(s.shape, s.dtype) for s in shapes),
        in_specs=[hbm_space] * 8,
        out_specs=[any_space] * 5,
        scratch_shapes=scratch,
        compiler_params=pltpu.CompilerParams(
            collective_id=0, has_side_effects=True, vmem_limit_bytes=VMEM_LIMIT
        ),
        cost_estimate=pl.CostEstimate(flops=4 * 2**30, bytes_accessed=4 * 2**20, transcendentals=0),
    )(inputs, w_value, q_field, k_field, filters, out_grad, jnp.asarray(forward), jnp.asarray(inverse))
    return pl.pallas_call(
        copy_kernel,
        out_shape=shapes,
        in_specs=[any_space] * 5,
        out_specs=[hbm_space] * 5,
        scratch_shapes=[pltpu.SemaphoreType.DMA((5,))],
        compiler_params=pltpu.CompilerParams(vmem_limit_bytes=8 * 1024 * 1024),
    )(*results)


def solution(mesh):
    return jax.shard_map(
        body,
        mesh=mesh,
        in_specs=(
            P("ctx", "chan"),
            P("ctx", "chan"),
            P("ctx", "chan"),
            P("ctx", "chan"),
            P(None, "chan"),
            P("ctx", "chan"),
        ),
        out_specs=(
            P("ctx", "chan"),
            P("ctx", "chan"),
            P("ctx", "chan"),
            P("ctx", "chan"),
            P(None, "chan"),
        ),
        check_vma=False,
    )
```

```python
import jax
import jax.numpy as jnp
import ml_dtypes
import numpy as np
from jax import lax
from jax.experimental import pallas as pl
from jax.experimental.pallas import tpu as pltpu
from jax.sharding import PartitionSpec as P

MESH = pl.DeviceIdType.MESH
F32, BF16 = jnp.float32, jnp.bfloat16
BLK = 128
CH = 512
NX, NY, NZ = 2, 4, 8
N_CTX = 2 * NZ * 2

R_IN1, R_IN2, R_WX, R_WR, R_WL = 0, 8, 14, 16, 32
R_H, R_G, R_V, R_VC, R_VX = 48, 49, 50, 57, 61
R_RS, R_RSX, R_WG, R_IG1, R_IG2 = 64, 78, 80, 81, 87
R_F1, R_F2, R_F3, R_F4 = 95, 98, 105, 112
N_RECV = 115
N_SEND = 140
N_LOCAL = 16
VMEM_LIMIT = 60 * 1024 * 1024


def transforms():
    k, n = np.arange(BLK)[:, None], np.arange(BLK)[None, :]
    angle = np.pi * (2 * k + 1) * n / (2 * BLK)
    full = np.concatenate([np.cos(angle), -np.sin(angle)], 0)
    high = full.astype(ml_dtypes.bfloat16)
    low = (full - high.astype(np.float64)).astype(ml_dtypes.bfloat16)
    forward = np.concatenate([high, low], 0)
    inverse = np.concatenate([high.T, low.T], 0).astype(np.float32) / BLK
    halves = np.concatenate([inverse[:, :BLK], inverse[:, BLK:]], 0)
    return forward, halves.astype(ml_dtypes.bfloat16)


def kernel(
    x_hbm, w_hbm, q_hbm, k_hbm, f_hbm, o_hbm, fwd_hbm, inv_hbm,
    ig_hbm, wg_hbm, qg_hbm, kg_hbm, fg_hbm,
    q_v, k_v, o_v, f_v, fwd_v, inv_v,
    h_v, hn_v, g_v, gp_v, fs_v, hs_v, gg_v,
    gin, wfull, vfull,
    rs_out, rs_in, rs_x, wx_s, wx_r,
    val_t, val_s, val_c, val_xs, val_xr,
    ig_s, ig_r, ig_sum,
    qg_v, kg_v, fq_s, fq_r, fz_s, fz_r, fz_all, fq_all, fg_v,
    wg_v,
    ssem, rsem, lsem,
):
    chan, ctx = lax.axis_index("chan"), lax.axis_index("ctx")
    xl, y = chan // NY, chan % NY
    xh, z, core = ctx // (2 * NZ), (ctx // 2) % NZ, ctx % 2
    tb = xh * 2 + core
    xo = 1 - xl

    def dev(xh_, xl_, y_, z_, core_):
        return (xl_ * NY + y_, xh_ * (2 * NZ) + z_ * 2 + core_)

    def bits(d):
        return (xh + d // 4) % 2, (xl + (d // 2) % 2) % 2, (core + d % 2) % 2

    def plane(d):
        xh_, xl_, core_ = bits(d)
        return dev(xh_, xl_, y, z, core_)

    def y_peer(d):
        return dev(xh, xl, (y + d) % NY, z, core)

    def z_peer(d):
        return dev(xh, xl, y, (z + d + NZ) % NZ, core)

    def z_partner(d):
        return dev(xh, xo, y, (z + d + NZ) % NZ, core)

    def ctx_peer(d):
        return (chan, (ctx + d + N_CTX) % N_CTX)

    right, left, partner, sibling = z_peer(1), z_peer(-1), plane(2), plane(1)
    started = []
    local_ids = iter(range(N_LOCAL))

    def send(src, dst, device, recv):
        copy = pltpu.make_async_remote_copy(
            src_ref=src, dst_ref=dst, send_sem=ssem.at[len(started)], recv_sem=rsem.at[recv],
            device_id=device, device_id_type=MESH,
        )
        copy.start()
        started.append(copy)

    def arrive(dst, recv):
        pltpu.make_async_copy(dst, dst, rsem.at[recv]).wait()

    def local(src, dst):
        copy = pltpu.make_async_copy(src, dst, lsem.at[next(local_ids)])
        copy.start()
        return copy

    def rows(index, size=BLK):
        return pl.ds(pl.multiple_of(index * size, size), size)

    def lanes(index, size=128):
        return pl.ds(pl.multiple_of(index * size, size), size)

    def dot(a, b):
        return jnp.dot(a, b, preferred_element_type=F32)

    def forward(block):
        t = dot(fwd_v[...], block)
        return t[:256] + t[256:]

    def inverse(re, im):
        spec = jnp.concatenate([re, im], 0)
        high = spec.astype(BF16)
        low = (spec - high.astype(F32)).astype(BF16)
        t = dot(inv_v[...], high)
        return t[:BLK] + t[BLK:] + dot(inv_v[:BLK], low)

    sign = (1 - 2 * (lax.broadcasted_iota(jnp.int32, (BLK, CH), 0) % 2)).astype(F32)

    loads = [local(a, b) for a, b in (
        (o_hbm, o_v), (q_hbm, q_v), (fwd_hbm, fwd_v), (f_hbm, f_v), (k_hbm, k_v),
        (inv_hbm.at[:256], inv_v.at[:, :BLK]), (inv_hbm.at[256:], inv_v.at[:, BLK:]))]
    w_local = local(w_hbm.at[rows(xl), :], wfull.at[xl, rows(z), :])
    barrier = pltpu.get_barrier_semaphore()
    greeted = [plane(d) for d in range(1, 8)] + [y_peer(d) for d in range(1, NY)]
    greeted += [z_peer(d) for d in range(1, NZ)] + [ctx_peer(1), ctx_peer(-1), z_partner(1), z_partner(-1)]
    for device in greeted:
        pl.semaphore_signal(barrier, inc=1, device_id=device, device_id_type=MESH)
    pl.semaphore_wait(barrier, len(greeted))

    def w_piece(stream, zz):
        return wfull.at[xl if stream < 2 else xo, rows(zz * 2 + stream % 2, 64), :]

    def w_start(stream, src):
        send(src, w_piece(stream, z), right, R_WR + stream * 4)
        send(src, w_piece(stream, z), left, R_WL + stream * 4)

    for part in range(2):
        send(w_hbm.at[rows(xo * 2 + part, 64), :], w_piece(part, z), partner, R_WX + part)
    for part in range(2):
        w_start(part, w_hbm.at[rows(xl * 2 + part, 64), :])

    def in_slab(b9, xl_, core_):
        return lanes(b9 * 4 + core_ * 2 + xl_)

    def gin_slab(place, b9):
        return gin.at[rows(place), lanes(y * 2 + b9)]

    self_sends = []

    def send_or_copy(src, dst, device, recv, same_x):
        if not same_x:
            return send(src, dst, device, recv)
        far = pltpu.make_async_remote_copy(
            src_ref=src, dst_ref=dst, send_sem=ssem.at[N_SEND - 1 - len(self_sends)], recv_sem=rsem.at[recv],
            device_id=device, device_id_type=MESH,
        )
        near = pltpu.make_async_copy(src, dst, rsem.at[recv])
        self_sends.append(far)

        @pl.when(xh != xl)
        def _():
            far.start()

        @pl.when(xh == xl)
        def _():
            near.start()

    for a in (1, 0):
        for b in (1, 0):
            xl_d, core_d = (xl + a) % 2, (core + b) % 2
            for b9 in range(2):
                src = x_hbm.at[:, in_slab(b9, xl_d, core_d)]
                send_or_copy(src, gin_slab(tb, b9), dev(xl, xl_d, y, z, core_d), R_IN1 + tb * 2 + b9, a + b == 0)

    loads[0].wait()
    loads[1].wait()
    h = (o_v[...].astype(F32) * q_v[...].astype(F32)).astype(BF16)
    h_v[...] = h
    send(h_v, hn_v, ctx_peer(-1), R_H)
    loads[2].wait()
    loads[3].wait()
    taps = f_v[...]
    taps_high = taps.astype(BF16)
    taps_low = (taps - taps_high.astype(F32)).astype(BF16)
    fs_v[...] = forward(taps_high) + dot(fwd_v[:256], taps_low)
    hs_v[...] = forward(h)

    def gin_part(place, yy):
        return gin.at[rows(place, 256), lanes(yy, 256)]

    def in_second(turn):
        place = (xl + turn) % 2
        for i in range(2):
            for b9 in range(2):
                arrive(gin_slab(place * 2 + i, b9), R_IN1 + (place * 2 + i) * 2 + b9)
        for d in (2, 1, 3):
            send(gin_part(place, y), gin_part(place, y), y_peer(d), R_IN2 + (d - 1) * 2 + place)

    def w_step(stream, k):
        for step, base, hops in ((1, R_WR, 4 - stream % 2), (-1, R_WL, 3 + stream % 2)):
            if k > hops:
                continue
            piece = w_piece(stream, (z - step * k + NZ) % NZ)
            arrive(piece, base + stream * 4 + k - 1)
            if k < hops:
                send(piece, piece, z_peer(step), base + stream * 4 + k)

    def w_own(k):
        w_step(0, k)
        w_step(1, k)

    def w_par(k):
        w_step(2, k)
        w_step(3, k)

    w_local.wait()
    w_own(1)
    for part in range(2):
        arrive(w_piece(2 + part, z), R_WX + part)
        w_start(2 + part, w_piece(2 + part, z))
    in_second(0)

    arrive(hn_v, R_H)
    for load in loads[4:]:
        load.wait()
    hn = forward(jnp.where(ctx == N_CTX - 1, jnp.zeros_like(h), hn_v[...]))
    hr = hs_v[:BLK] + sign * hn[BLK:]
    hi = hs_v[BLK:] - sign * hn[:BLK]
    hs_v[:BLK] = hr
    hs_v[BLK:] = hi
    fr, fi = fs_v[:BLK], fs_v[BLK:]
    g_grad = inverse(fr * hr + fi * hi, fr * hi - fi * hr)
    gg_v[...] = g_grad
    vfull[xl, rows(tb), :] = (g_grad * k_v[...].astype(F32)).astype(BF16)

    def v_piece(d):
        xh_, xl_, core_ = bits(d)
        return vfull.at[xl_, rows(xh_ * 2 + core_), :]

    for d in (4, 6, 2, 1):
        send(v_piece(0), v_piece(0), plane(d), R_V + d - 1)
    in_second(1)
    w_own(2)
    w_par(1)
    w_own(3)
    w_par(2)
    for d in (2, 6, 4):
        arrive(v_piece(d), R_V + d - 1)
        send(v_piece(d), v_piece(d), sibling, R_V + d)
    w_own(4)
    w_par(3)
    for d in (1, 3, 5, 7):
        arrive(v_piece(d), R_V + d - 1)
    for place in range(2):
        for d in range(1, NY):
            arrive(gin_part(place, (y - d + NY) % NY), R_IN2 + (d - 1) * 2 + place)

    def w_term(zz, half):
        return lax.dot_general(
            gin[:, lanes(zz)], vfull[half], (((0,), (0,)), ((), ())), preferred_element_type=F32
        )

    def rs_step(i):
        hop = 4 - (i + 1) // 2
        for way, step in ((0, 1), (1, -1)):
            own = (i + way) % 2 == 0
            term = w_term((z + step * hop + NZ) % NZ, xl if own else xo)
            if i >= 2:
                arrive(rs_in.at[way, i - 2], R_RS + way * 7 + i - 2)
                term = term + rs_in[way, i - 2].astype(F32)
            rs_out[way, i] = term.astype(BF16)
            if hop == 1 and not own:
                send(rs_out.at[way, i], rs_x.at[way], z_partner(step), R_RSX + way)
            else:
                send(rs_out.at[way, i], rs_in.at[way, i], z_peer(step), R_RS + way * 7 + i)

    rs_step(0)
    rs_step(1)

    def val_part(j):
        xh_d, xl_d, _ = bits(2 * j)
        val_t[j] = dot(gin[rows(xh_d, 256), :], wfull[xl_d])
        val_s[j] = val_t[j, rows(1 - core), :].astype(BF16)
        send(val_s.at[j], val_c.at[j], sibling, R_VC + j)

    def val_send(j):
        arrive(val_c.at[j], R_VC + j)
        val_xs[j - 1] = (val_t[j, rows(core), :] + val_c[j].astype(F32)).astype(BF16)
        send(val_xs.at[j - 1], val_xr.at[j - 1], plane(2 * j), R_VX + j - 1)

    val_part(2)
    val_part(0)
    val_send(2)
    w_par(4)
    val_part(1)
    val_part(3)
    val_send(1)
    val_send(3)
    rs_step(2)

    def in_term(place, yy):
        total = 0.0
        for half in range(2):
            total = total + lax.dot_general(
                vfull[half, rows(place, 256), :], wfull[half, rows(yy, 256), :], (((1,), (1,)), ((), ())),
                preferred_element_type=F32,
            )
        return total

    def ig_first(turn):
        place = (xo + turn) % 2
        for d in (2, 1, 3):
            slot = (d - 1) * 2 + turn
            ig_s[slot] = in_term(place, (y + d) % NY).astype(BF16)
            send(ig_s.at[slot], ig_r.at[slot], y_peer(d), R_IG1 + slot)

    def ig_second(turn):
        place = (xo + turn) % 2
        total = in_term(place, y)
        for d in (1, 3, 2):
            slot = (d - 1) * 2 + turn
            arrive(ig_r.at[slot], R_IG1 + slot)
            total = total + ig_r[slot].astype(F32)
        ig_sum[turn] = total.astype(BF16)
        for b in (1, 0):
            core_d = (core + b) % 2
            for b9 in range(2):
                src = ig_sum.at[turn, rows(core_d), b9 * 128 : (b9 + 1) * 128]
                dst = ig_hbm.at[:, in_slab(b9, xl, core)]
                send_or_copy(src, dst, dev(place, xh, y, z, core_d), R_IG2 + (xl * 2 + core) * 2 + b9, turn + b == 1 and b == 0)

    ig_first(0)
    ig_first(1)

    arrive(val_c.at[0], R_VC)
    value = val_t[0, rows(core), :] + val_c[0].astype(F32)
    for j in (2, 1, 3):
        arrive(val_xr.at[j - 1], R_VX + j - 1)
        value = value + val_xr[j - 1].astype(F32)
    value = value.astype(BF16).astype(F32)
    gated = (k_v[...].astype(F32) * value).astype(BF16)
    g_v[...] = gated
    send(g_v, gp_v, ctx_peer(1), R_G)
    own = forward(gated)
    hr, hi = hs_v[:BLK], hs_v[BLK:]
    filter_part = inverse(own[:BLK] * hr + own[BLK:] * hi, own[:BLK] * hi - own[BLK:] * hr)
    fg_v[...] = filter_part

    for i in range(4):
        fq_s[i] = filter_part[:, i * 128 : (i + 1) * 128].astype(BF16)
    group = ((1, 1), (2, 4), (3, 5))
    for place, d in group:
        xh_d, _, core_d = bits(d)
        send(fq_s.at[xh_d * 2 + core_d], fq_r.at[place - 1], plane(d), R_F1 + place - 1)
    kg_v[...] = (gg_v[...] * value).astype(BF16)
    outs = [local(kg_v, kg_hbm)]
    rs_step(3)
    rs_step(4)
    wx_s[...] = w_term(z, xo).astype(BF16)
    send(wx_s, wx_r, partner, R_WG)

    total = fg_v[:, lanes(tb)]
    for place in range(3):
        arrive(fq_r.at[place], R_F1 + place)
        total = total + fq_r[place].astype(F32)
    fg_v[:, :128] = total
    for i in range(NZ):
        fz_s[i] = total[i * 16 : (i + 1) * 16].astype(BF16)
    for d in range(1, NZ):
        send(fz_s.at[(z + d) % NZ], fz_r.at[d - 1], z_peer(d), R_F2 + d - 1)
    rs_step(5)
    ig_second(0)

    arrive(gp_v, R_G)
    before = forward(jnp.where(ctx == 0, jnp.zeros_like(gated), gp_v[...]))
    er = own[:BLK] - sign * before[BLK:]
    ei = own[BLK:] + sign * before[:BLK]
    fr, fi = fs_v[:BLK], fs_v[BLK:]
    filtered = inverse(fr * er - fi * ei, fr * ei + fi * er)
    qg_v[...] = (o_v[...].astype(F32) * filtered).astype(BF16)
    outs.append(local(qg_v, qg_hbm))

    piece = fg_v[rows(z, 16), :128]
    for d in range(1, NZ):
        arrive(fz_r.at[d - 1], R_F2 + d - 1)
        piece = piece + fz_r[d - 1].astype(F32)
    fz_all[z] = piece.astype(BF16)
    for d in range(1, NZ):
        send(fz_all.at[z], fz_all.at[z], z_peer(d), R_F3 + d - 1)
    rs_step(6)
    ig_second(1)

    for d in range(1, NZ):
        arrive(fz_all.at[(z - d + NZ) % NZ], R_F3 + d - 1)
    for i in range(NZ):
        fq_all[tb, i * 16 : (i + 1) * 16, :] = fz_all[i]
    for place, d in group:
        send(fq_all.at[tb], fq_all.at[tb], plane(d), R_F4 + place - 1)

    term = w_term(z, xl)
    arrive(rs_in.at[1, 5], R_RS + 7 + 5)
    term = term + rs_in[1, 5].astype(F32)
    arrive(wx_r, R_WG)
    arrive(rs_x.at[0], R_RSX)
    other = wx_r[...].astype(F32) + rs_x[0].astype(F32)
    arrive(rs_in.at[0, 6], R_RS + 6)
    wg_v[0] = (term + rs_in[0, 6].astype(F32)).astype(BF16)
    outs.append(local(wg_v.at[0], wg_hbm.at[rows(xl), :]))
    arrive(rs_x.at[1], R_RSX + 1)
    wg_v[1] = (other + rs_x[1].astype(F32)).astype(BF16)
    outs.append(local(wg_v.at[1], wg_hbm.at[rows(xo), :]))

    for place, d in group:
        xh_s, _, core_s = bits(d)
        arrive(fq_all.at[xh_s * 2 + core_s], R_F4 + place - 1)
    for i in range(4):
        fg_v[:, i * 128 : (i + 1) * 128] = fq_all[i].astype(F32)
    outs.append(local(fg_v, fg_hbm))

    for xl_s in range(2):
        for core_s in range(2):
            for b9 in range(2):
                arrive(ig_hbm.at[:, in_slab(b9, xl_s, core_s)], R_IG2 + (xl_s * 2 + core_s) * 2 + b9)
    for copy in started:
        copy.wait_send()

    @pl.when(xh != xl)
    def _():
        for copy in self_sends:
            copy.wait_send()

    for copy in outs:
        copy.wait()


def copy_kernel(*refs):
    sources, targets, sem = refs[:5], refs[5:10], refs[10]
    copies = [pltpu.make_async_copy(a, b, sem.at[i]) for i, (a, b) in enumerate(zip(sources, targets))]
    for copy in copies:
        copy.start()
    for copy in copies:
        copy.wait()


def body(inputs, w_value, q_field, k_field, filters, out_grad):
    forward, inverse = transforms()
    blk = (BLK, CH)
    vmem = pltpu.VMEM
    scratch = [
        vmem(blk, BF16), vmem(blk, BF16), vmem(blk, BF16), vmem(blk, F32),
        vmem((512, BLK), BF16), vmem((256, 256), BF16),
        vmem(blk, BF16), vmem(blk, BF16), vmem(blk, BF16), vmem(blk, BF16),
        vmem((256, CH), F32), vmem((256, CH), F32), vmem(blk, F32),
        vmem((512, 1024), BF16), vmem((2, 1024, CH), BF16), vmem((2, 512, CH), BF16),
        vmem((2, 7) + blk, BF16), vmem((2, 7) + blk, BF16), vmem((2,) + blk, BF16),
        vmem(blk, BF16), vmem(blk, BF16),
        vmem((4, 256, CH), F32), vmem((4,) + blk, BF16), vmem((4,) + blk, BF16),
        vmem((3,) + blk, BF16), vmem((3,) + blk, BF16),
        vmem((6, 256, 256), BF16), vmem((6, 256, 256), BF16), vmem((2, 256, 256), BF16),
        vmem(blk, BF16), vmem(blk, BF16),
        vmem((4, BLK, 128), BF16), vmem((3, BLK, 128), BF16),
        vmem((NZ, 16, 128), BF16), vmem((NZ - 1, 16, 128), BF16), vmem((NZ, 16, 128), BF16),
        vmem((4, BLK, 128), BF16), vmem(blk, F32),
        vmem((2,) + blk, BF16),
        pltpu.SemaphoreType.DMA((N_SEND,)),
        pltpu.SemaphoreType.DMA((N_RECV,)),
        pltpu.SemaphoreType.DMA((N_LOCAL,)),
    ]
    any_space = pl.BlockSpec(memory_space=pl.ANY)
    hbm_space = pl.BlockSpec(memory_space=pltpu.HBM)
    shapes = (
        jax.ShapeDtypeStruct((BLK, 1024), BF16),
        jax.ShapeDtypeStruct((256, CH), BF16),
        jax.ShapeDtypeStruct(blk, BF16),
        jax.ShapeDtypeStruct(blk, BF16),
        jax.ShapeDtypeStruct(blk, F32),
    )
    results = pl.pallas_call(
        kernel,
        out_shape=tuple(vmem(s.shape, s.dtype) for s in shapes),
        in_specs=[hbm_space] * 8,
        out_specs=[any_space] * 5,
        scratch_shapes=scratch,
        compiler_params=pltpu.CompilerParams(
            collective_id=0, has_side_effects=True, vmem_limit_bytes=VMEM_LIMIT
        ),
        cost_estimate=pl.CostEstimate(flops=4 * 2**30, bytes_accessed=4 * 2**20, transcendentals=0),
    )(inputs, w_value, q_field, k_field, filters, out_grad, jnp.asarray(forward), jnp.asarray(inverse))
    return pl.pallas_call(
        copy_kernel,
        out_shape=shapes,
        in_specs=[any_space] * 5,
        out_specs=[hbm_space] * 5,
        scratch_shapes=[pltpu.SemaphoreType.DMA((5,))],
        compiler_params=pltpu.CompilerParams(vmem_limit_bytes=8 * 1024 * 1024),
    )(*results)


def solution(mesh):
    return jax.shard_map(
        body,
        mesh=mesh,
        in_specs=(
            P("ctx", "chan"),
            P("ctx", "chan"),
            P("ctx", "chan"),
            P("ctx", "chan"),
            P(None, "chan"),
            P("ctx", "chan"),
        ),
        out_specs=(
            P("ctx", "chan"),
            P("ctx", "chan"),
            P("ctx", "chan"),
            P("ctx", "chan"),
            P(None, "chan"),
        ),
        check_vma=False,
    )
```
